256 devices in a mesh: prompt: 16 (over x, y), comp: 16 (over z, core).
Axes of the slice: x: 4, y: 4, z: 8, core: 2. Of those that a mesh axis runs over, the one named last changes fastest.
Arguments:
- q_raw: bfloat16 [16, 2048, 8192], P('prompt', 'comp'), may hold values from -8 to 8
- d_out: bfloat16 [16, 2048, 8192], P('prompt', 'comp'), may hold values from -6 to 6
- k_prompt: bfloat16 [16, 1024, 1024], P('prompt', 'comp'), may hold values from -8 to 8
- v_prompt: bfloat16 [16, 1024, 1024], P('prompt', 'comp'), may hold values from -6 to 6
- k_comp: bfloat16 [16, 2048, 1024], P('prompt', 'comp'), may hold values from -6 to 6
- v_comp: bfloat16 [16, 2048, 1024], P('prompt', 'comp'), may hold values from -6 to 6
- lengths: int32 [16, 16, 4], P('prompt', 'comp'), may hold values from 1 to 64, 128 in all within a row
- q_gain: float32 [128], replicated, may hold values from 0.5 to 4.5
- k_gain: float32 [128], replicated, may hold values from 0.5 to 4.5
Outputs:
- d_q_raw: bfloat16 [16, 2048, 8192], P('prompt', 'comp')
- d_k_comp: bfloat16 [16, 2048, 1024], P('prompt', 'comp')
- d_v_comp: bfloat16 [16, 2048, 1024], P('prompt', 'comp')
- d_k_prompt: bfloat16 [16, 1024, 1024], P('prompt', 'comp')
- d_v_prompt: bfloat16 [16, 1024, 1024], P('prompt', 'comp')
- d_q_gain: float32 [128], replicated
- d_k_gain: float32 [128], replicated
The draws below stay inside these ranges and needn't reach their ends.
Inputs may be any that keep to these rules, and one draw needn't show every extreme that they name: Each row of lengths sums to 128, and its largest entry is 64.
All inputs are finite; a program needn't handle non-finite values.
Results may differ from the reference program's by a relative error of at most 0.027.
The reference program's roundings to bfloat16 on the way count: a program that leaves them out, or rounds other values in their place, can miss the bound.
Values may be sent and summed in bfloat16 or wider, within the bound.
A program may use at most 128 MiB of HBM per device.

```python
import math
import jax
import jax.numpy as jnp
import numpy as np
from jax import lax

H = 64
KVH = 8
HD = 128
SLOTS = 128
CPD = 4
PL = 1024
TOKS = 2048
N_PROMPT = 16
N_COMP = 16


def prompt_keys(key):
    return jnp.clip(jax.random.normal(key, (N_PROMPT, PL, KVH * HD), jnp.float32), -6.0, 6.0)


def draw_k_prompt(key, part):
    return prompt_keys(key).astype(jnp.bfloat16)


def draw_q_raw(key, part):
    key = jax.random.fold_in(key, 11)
    values = jax.random.normal(key, (N_PROMPT, TOKS, H * HD), jnp.float32)
    return jnp.clip(values, -6.0, 6.0).astype(jnp.bfloat16)


def draw_q_gain(key, part):
    key = jax.random.fold_in(key, 21)
    return jnp.exp(jax.random.uniform(key, (HD,), jnp.float32, math.log(0.5), math.log(1.5)))


def draw_k_gain(key, part):
    key = jax.random.fold_in(key, 31)
    return jnp.exp(jax.random.uniform(key, (HD,), jnp.float32, math.log(0.5), math.log(1.5)))


def level_of(rng, shape, split, smallest, high):
    def one(position, shards_of):
        heights = jax.random.uniform(jax.random.fold_in(jax.random.fold_in(rng, 6), position), (shards_of,), jnp.float32, smallest / len(split), high / len(split))
        return jnp.repeat(jnp.exp(heights), shape[position] // shards_of).reshape((-1,) + (1,) * (len(shape) - position - 1))

    level = one(*split[0])
    for cut in split[1:]:
        level = level * one(*cut)
    return level


def split_up(amount, total, most, skew):
    portions = [(1 << 20) // math.isqrt(standing ** skew) + 1 for standing in range(2, amount + 1)]
    surplus, counts = total - most - (amount - 1), [1] * (amount - 1)
    while surplus > 0:
        free = [i for i in range(amount - 1) if counts[i] < most]
        pool, left = sum([portions[i] for i in free]), surplus
        for i in free:
            more = min(most - counts[i], max(1, left * portions[i] // pool), surplus)
            counts[i] = counts[i] + more
            surplus = surplus - more
    return np.array([most] + counts)


def uneven(key, count, total, most, slope):
    if count == 2:
        one = jax.random.randint(key, (), max(1, total - most), min(most, total - 1) + 1)
        return jnp.stack([one, total - one])
    sizes = jnp.asarray(split_up(count, total, most, slope), jnp.int32)
    couples = (count - 1) // 2
    donor, sink = sizes[1:1 + 2 * couples:2], sizes[2:2 + 2 * couples:2]
    margin = jnp.minimum(donor - 1, most - sink)
    moved = jax.random.randint(jax.random.fold_in(key, 1), (couples,), 0, 1 << 20) % (margin + 1)
    sizes = sizes.at[1:1 + 2 * couples:2].set(donor - moved).at[2:2 + 2 * couples:2].set(sink + moved)
    return sizes[jax.random.permutation(jax.random.fold_in(key, 2), count)]


def scatter_about(rng, dims, scale, limit, pieces=(), kind=jnp.bfloat16):
    result = scale * jax.random.normal(rng, dims, jnp.float32)
    if pieces:
        result = result * level_of(rng, dims, pieces, -0.22, 0.18)
    return jnp.clip(result, -limit, limit).astype(kind)


def setup_inputs(seed: int = 0) -> dict:
    key_list = jax.random.split(jax.random.key(seed), 10)
    q_raw = draw_q_raw(jax.random.fold_in(key_list[9], 71), 0)
    d_out = scatter_about(key_list[1], (N_PROMPT, TOKS, H * HD), 1.0, 6.0, ((0, 16), (1, 16)))
    k_prompt = draw_k_prompt(jax.random.fold_in(key_list[9], 71), 0)
    v_prompt = scatter_about(key_list[3], (N_PROMPT, PL, KVH * HD), 1.0, 6.0, ((0, 16), (1, 16)))
    k_comp = scatter_about(key_list[4], (N_PROMPT, TOKS, KVH * HD), 1.0, 6.0, ((0, 16), (1, 16)))
    v_comp = scatter_about(key_list[5], (N_PROMPT, TOKS, KVH * HD), 1.0, 6.0, ((0, 16), (1, 16)))
    lengths = jax.vmap(lambda own: uneven(own, CPD, SLOTS, SLOTS // 2, 2))(jax.random.split(key_list[6], N_PROMPT * N_COMP)).reshape((N_PROMPT, N_COMP, CPD)).astype(jnp.int32)
    q_gain = draw_q_gain(jax.random.fold_in(key_list[9], 71), 0)
    k_gain = draw_k_gain(jax.random.fold_in(key_list[9], 71), 0)
    return dict(q_raw=q_raw, d_out=d_out, k_prompt=k_prompt, v_prompt=v_prompt, k_comp=k_comp, v_comp=v_comp, lengths=lengths, q_gain=q_gain, k_gain=k_gain)


epsilon = 1e-06

def norm_rows(values, gain):
    values = values.astype(jnp.float32)
    inverse = lax.rsqrt(lax.optimization_barrier(jnp.mean(values * values, axis=-1, keepdims=True)) + epsilon)
    return (values * inverse * gain, inverse)

def norm_back(values, inverse, gain, grad):
    values = values.astype(jnp.float32)
    scaled = grad * gain
    inner = lax.optimization_barrier(jnp.mean(values * scaled, axis=-1, keepdims=True))
    dx = inverse * scaled - values * inverse * inverse * inverse * inner
    dgain = lax.optimization_barrier(jnp.sum((grad * values * inverse).reshape(-1, values.shape[-1]), axis=0))
    return (dx, dgain)

def segment_ids(lengths, slots):
    ends = jnp.cumsum(lengths).astype(jnp.int32)
    places = jnp.arange(slots, dtype=jnp.int32)
    return lax.optimization_barrier(jnp.sum((places[:, None] >= ends[None, :]).astype(jnp.int32), axis=1)).astype(jnp.int32)

def block_grads(q_block, grad_block, k_prefix, v_prefix, k_own, v_own, lens, q_gain, k_gain):
    group = H // KVH
    scale = 1.0 / math.sqrt(HD)
    f32 = jnp.float32
    query_raw = q_block.reshape(SLOTS, KVH, group, HD)
    query_norm, query_inv = norm_rows(query_raw, q_gain)
    query = query_norm.astype(jnp.bfloat16).astype(f32)
    prefix_keys = norm_rows(k_prefix.reshape(PL, KVH, HD), k_gain)[0].astype(jnp.bfloat16).astype(f32)
    own_raw = k_own.reshape(SLOTS, KVH, HD)
    own_norm, own_inv = norm_rows(own_raw, k_gain)
    own_keys = own_norm.astype(jnp.bfloat16).astype(f32)
    prefix_vals = v_prefix.reshape(PL, KVH, HD).astype(f32)
    own_vals = v_own.reshape(SLOTS, KVH, HD).astype(f32)
    grad_out = grad_block.reshape(SLOTS, KVH, group, HD).astype(f32)
    seg = segment_ids(lens, SLOTS)
    places = jnp.arange(SLOTS, dtype=jnp.int32)
    visible = (seg[:, None] == seg[None, :]) & (places[None, :] <= places[:, None])
    score_p = jnp.einsum('sjgd,tjd->jgst', query, prefix_keys) * scale
    score_c = jnp.einsum('sjgd,tjd->jgst', query, own_keys) * scale
    top = jnp.maximum(lax.optimization_barrier(jnp.max(score_p, axis=-1)), lax.optimization_barrier(jnp.max(jnp.where(visible, score_c, -1e+30), axis=-1)))
    total = lax.optimization_barrier(jnp.sum(jnp.exp(score_p - top[..., None]), axis=-1))
    total = total + lax.optimization_barrier(jnp.sum(jnp.where(visible, jnp.exp(score_c - top[..., None]), 0.0), axis=-1))
    lse = top + jnp.log(total)
    prob_p = jnp.exp(score_p - lse[..., None])
    prob_c = jnp.where(visible, jnp.exp(score_c - lse[..., None]), 0.0)
    probb_p = prob_p.astype(jnp.bfloat16).astype(f32)
    probb_c = prob_c.astype(jnp.bfloat16).astype(f32)
    output = jnp.einsum('jgst,tjd->sjgd', probb_p, prefix_vals) + jnp.einsum('jgst,tjd->sjgd', probb_c, own_vals)
    delta = jnp.transpose(lax.optimization_barrier(jnp.sum(grad_out * output, axis=-1)), (1, 2, 0))
    dprob_p = jnp.einsum('sjgd,tjd->jgst', grad_out, prefix_vals)
    dprob_c = jnp.einsum('sjgd,tjd->jgst', grad_out, own_vals)
    dsb_p = (prob_p * (dprob_p - delta[..., None])).astype(jnp.bfloat16).astype(f32)
    dsb_c = (prob_c * (dprob_c - delta[..., None])).astype(jnp.bfloat16).astype(f32)
    d_query = (jnp.einsum('jgst,tjd->sjgd', dsb_p, prefix_keys) + jnp.einsum('jgst,tjd->sjgd', dsb_c, own_keys)) * scale
    dk_prefix = jnp.einsum('jgst,sjgd->tjd', dsb_p, query) * scale
    dv_prefix = jnp.einsum('jgst,sjgd->tjd', probb_p, grad_out)
    dk_own = jnp.einsum('jgst,sjgd->tjd', dsb_c, query) * scale
    dv_own = jnp.einsum('jgst,sjgd->tjd', probb_c, grad_out)
    dq_raw, gain_q = norm_back(query_raw, query_inv, q_gain, d_query)
    dk_raw, gain_k = norm_back(own_raw, own_inv, k_gain, dk_own)
    return (dq_raw.reshape(SLOTS, H * HD).astype(jnp.bfloat16), dk_raw.reshape(SLOTS, KVH * HD).astype(jnp.bfloat16), dv_own.reshape(SLOTS, KVH * HD).astype(jnp.bfloat16), dk_prefix, dv_prefix, gain_q, gain_k)

def reference(q_raw, d_out, k_prompt, v_prompt, k_comp, v_comp, lengths, q_gain, k_gain):

    def one_group(items):
        q_group, grad_group, kp_group, vp_group, kc_group, vc_group, len_group = items

        def one_block(carry, inner):
            q_block, grad_block, kc_block, vc_block, lens = inner
            res = block_grads(q_block, grad_block, kp_group, vp_group, kc_block, vc_block, lens, q_gain, k_gain)
            carry = (carry[0] + res[3], carry[1] + res[4], carry[2] + res[5], carry[3] + res[6])
            return (carry, (res[0], res[1], res[2]))
        start = (jnp.zeros((PL, KVH, HD), jnp.float32), jnp.zeros((PL, KVH, HD), jnp.float32), jnp.zeros((HD,), jnp.float32), jnp.zeros((HD,), jnp.float32))
        inner = (q_group.reshape(N_COMP, SLOTS, H * HD), grad_group.reshape(N_COMP, SLOTS, H * HD), kc_group.reshape(N_COMP, SLOTS, KVH * HD), vc_group.reshape(N_COMP, SLOTS, KVH * HD), len_group)
        carry, blocks = lax.scan(one_block, start, inner)
        prefix_raw = kp_group.reshape(PL, KVH, HD)
        prefix_inv = norm_rows(prefix_raw, k_gain)[1]
        dk_prefix, gain_kp = norm_back(prefix_raw, prefix_inv, k_gain, carry[0])
        return (blocks[0].reshape(TOKS, H * HD), blocks[1].reshape(TOKS, KVH * HD), blocks[2].reshape(TOKS, KVH * HD), dk_prefix.reshape(PL, KVH * HD).astype(jnp.bfloat16), carry[1].reshape(PL, KVH * HD).astype(jnp.bfloat16), carry[2], carry[3] + gain_kp)
    res = lax.map(one_group, (q_raw, d_out, k_prompt, v_prompt, k_comp, v_comp, lengths))
    return (res[0], res[1], res[2], res[3], res[4], lax.optimization_barrier(jnp.sum(res[5], axis=0)), lax.optimization_barrier(jnp.sum(res[6], axis=0)))
```

```python
import functools
import math

import jax
import jax.numpy as jnp
from jax import lax
from jax.experimental import pallas as pl
from jax.experimental.pallas import tpu as pltpu
from jax.sharding import PartitionSpec as P

MESH = pl.DeviceIdType.MESH
f32 = jnp.float32
bf16 = jnp.bfloat16
KVH = 8
GRP = 8
HD = 128
SLOTS = 128
PL = 1024
KEYS = PL + SLOTS
ROWS = GRP * SLOTS
PAGE = 64
NZ = 8
NB = 16
CH = 256
TILE = 128
NT_ = KEYS // TILE
EPS = 1e-6
SCALE = 1.0 / math.sqrt(HD)
LOG2 = SCALE * math.log2(math.e)
FILL = 5
TICKS = FILL + KVH + 5

NT = (((1,), (1,)), ((), ()))
NN = (((1,), (0,)), ((), ()))


def dot(a, b, dims):
    return lax.dot_general(a, b, dims, preferred_element_type=f32)


def fold(x, op):
    return op(x.reshape(x.shape[0] // 8, 8, x.shape[1]), axis=0)


def cols(h, i=0, n=1):
    return pl.ds(pl.multiple_of(h * (n * HD) + i * HD, HD), HD)


def inv_rms(x):
    return lax.rsqrt(jnp.mean(x * x, axis=-1, keepdims=True) + EPS)


def norm_grad(x, gain, dy):
    r = inv_rms(x)
    xr = x * r
    u = dy * gain
    dx = r * (u - xr * jnp.mean(xr * u, axis=-1, keepdims=True))
    return dx, dy * xr


def remote(src, dst, send, recv, device):
    return pltpu.make_async_remote_copy(
        src_ref=src, dst_ref=dst, send_sem=send, recv_sem=recv, device_id=device, device_id_type=MESH
    )


def kernel(
    q_hbm, do_hbm, kp, vp, kc, vc, lens, qg, kg,
    dq_hbm, dkc, dvc, dkp, dvp, gains,
    qv, dov, dqv, qn, okn, vis, kvb, sc, dp, pb, ds, acc, sib, rsr, rss, gq, gk, gsend, grecv,
    q_sem, do_sem, dq_sem, ag_s, ag_b, ag_r, sl_s, sl_r, rs_s, rs_r, g_s, g_r,
):
    p = lax.axis_index("prompt")
    me = lax.axis_index("comp")
    z, c = me // 2, me % 2
    px, py = p // 4, p % 4
    zmod = lambda v: lax.rem(v + 2 * NZ, NZ)
    zdev = lambda v: {"comp": zmod(v) * 2 + c}
    sibling = {"comp": z * 2 + (1 - c)}
    mine = c * NZ + z
    theirs = (1 - c) * NZ
    stages = (
        [(1, c, sibling)],
        [(8, z, zdev(z + i)) for i in range(1, 8)],
        [(4, px, {"prompt": lax.rem(px + i, 4) * 4 + py}) for i in range(1, 4)],
        [(4, py, {"prompt": px * 4 + lax.rem(py + i, 4)}) for i in range(1, 4)],
    )

    barrier = pltpu.get_barrier_semaphore()
    for stage in stages:
        for _, _, dev in stage:
            pl.semaphore_signal(barrier, inc=1, device_id=dev, device_id_type=MESH)

    quarter = ROWS * 2
    for i in range(4):
        part = pl.ds(i * quarter, quarter)
        pltpu.make_async_copy(q_hbm.at[:, part], qv.at[:, part], q_sem.at[i]).start()
    pltpu.make_async_copy(do_hbm, dov, do_sem).start()

    for h in range(KVH):
        x = kp[:, h * HD : (h + 1) * HD].astype(f32)
        kvb[h, mine, 0] = (x * inv_rms(x) * kg[...]).astype(bf16)
        kvb[h, mine, 1] = vp[:, h * HD : (h + 1) * HD]
        x = kc[:, h * HD : (h + 1) * HD].astype(f32)
        okn[h] = (x * inv_rms(x) * kg[...]).astype(bf16)
    gq[...] = jnp.zeros_like(gq)
    gk[...] = jnp.zeros_like(gk)
    t_at = lax.broadcasted_iota(jnp.int32, (SLOTS, SLOTS), 0)
    s_at = lax.broadcasted_iota(jnp.int32, (SLOTS, SLOTS), 1)
    seg_t = jnp.zeros((SLOTS, SLOTS), jnp.int32)
    seg_s = jnp.zeros((SLOTS, SLOTS), jnp.int32)
    end = jnp.zeros((1, 1), jnp.int32)
    for i in range(4):
        end = end + lens[0:1, i : i + 1]
        seg_t += (t_at >= end).astype(jnp.int32)
        seg_s += (s_at >= end).astype(jnp.int32)
    seen = ((seg_t == seg_s) & (t_at <= s_at)).astype(f32)
    vis[...] = jnp.concatenate([seen] * (CH // SLOTS), axis=1)

    pl.semaphore_wait(barrier, sum(len(s) for s in stages))

    def between(v, lo, hi):
        return jnp.logical_and(v >= lo, v < hi)

    def block(h, slot, send, recv_slot_sem, dev):
        return remote(kvb.at[h, slot], kvb.at[h, slot], send, recv_slot_sem, dev)

    def gather(tick):
        h0 = tick

        @pl.when(between(h0, 0, KVH))
        def _():
            rsem = ag_r.at[h0, mine]
            block(h0, mine, ag_s.at[h0, 0, 0], rsem, zdev(z + 1)).start()
            block(h0, mine, ag_s.at[h0, 1, 0], rsem, zdev(z - 1)).start()
            block(h0, mine, ag_b.at[h0, 0], rsem, sibling).start()

        for k in (1, 2, 3):
            h = tick - k

            @pl.when(between(h, 0, KVH))
            def _(h=h, k=k):
                odd = lax.rem(h, 2)
                for d in (0, 1):
                    step = 1 - 2 * d
                    slot = c * NZ + zmod(z - step * k)
                    rsem = ag_r.at[h, slot]
                    block(h, slot, ag_b.at[h, 0], rsem, sibling).wait_recv()
                    if k < 3:
                        block(h, slot, ag_s.at[h, d, k], rsem, zdev(z + step)).start()
                    block(h, slot, ag_b.at[h, 1 + 3 * d + k - 1], rsem, sibling).start()
                if k == 3:
                    step = 1 - 2 * odd
                    slot = c * NZ + zmod(z - step * 3)
                    block(h, slot, ag_s.at[h, odd, 3], ag_r.at[h, slot], zdev(z + step)).start()

        h4 = tick - 4

        @pl.when(between(h4, 0, KVH))
        def _():
            slot = c * NZ + zmod(z + 4)
            rsem = ag_r.at[h4, slot]
            block(h4, slot, ag_b.at[h4, 7], rsem, sibling).wait_recv()
            block(h4, slot, ag_b.at[h4, 7], rsem, sibling).start()

    def prepare(h):
        for g in range(GRP):
            x = qv[:, cols(h, g, GRP)].astype(f32)
            qn[h, g * SLOTS : (g + 1) * SLOTS] = (x * inv_rms(x) * qg[...]).astype(bf16)

    def compute(h):
        for i in range(NZ):
            slot = theirs + i
            block(h, slot, ag_b.at[h, 0], ag_r.at[h, slot], sibling).wait_recv()

        def keys(t):
            return okn[h] if t == NT_ - 1 else kvb[h, 2 * t : 2 * t + 2, 0].reshape(TILE, HD)

        def vals(t):
            return vc[:, cols(h)] if t == NT_ - 1 else kvb[h, 2 * t : 2 * t + 2, 1].reshape(TILE, HD)

        grads = jnp.concatenate([dov[:, cols(h, g, GRP)] for g in range(GRP)], axis=0)
        for lo in range(0, ROWS, CH):
            at = slice(lo, lo + CH)
            qc = qn[h, at]
            gc = grads[at]
            top = None
            for t in range(NT_):
                ts = slice(t * TILE, (t + 1) * TILE)
                s = dot(keys(t), qc, NT)
                if t == NT_ - 1:
                    s = jnp.where(vis[...] > 0, s, -1e30)
                sc[ts, at] = s
                part = fold(s, jnp.max)
                top = part if top is None else jnp.maximum(top, part)
            top = jnp.max(top, axis=0, keepdims=True) * LOG2
            total = None
            for t in range(NT_):
                ts = slice(t * TILE, (t + 1) * TILE)
                e = jnp.exp2(sc[ts, at] * LOG2 - top)
                sc[ts, at] = e
                part = fold(e, jnp.sum)
                total = part if total is None else total + part
            inv = 1.0 / jnp.sum(total, axis=0, keepdims=True)
            delta = None
            for t in range(NT_):
                ts = slice(t * TILE, (t + 1) * TILE)
                d = dot(vals(t), gc, NT)
                dp[ts, at] = d
                b = (sc[ts, at] * inv).astype(bf16)
                pb[ts, at] = b
                part = fold(b.astype(f32) * d, jnp.sum)
                delta = part if delta is None else delta + part
            delta = jnp.sum(delta, axis=0, keepdims=True)
            for t in range(NT_):
                ts = slice(t * TILE, (t + 1) * TILE)
                ds[ts, at] = (sc[ts, at] * inv * (dp[ts, at] - delta)).astype(bf16)
        dv = dot(pb[...], grads, NN)
        dk = dot(ds[...], qn[h], NN) * SCALE
        gk_terms = jnp.zeros((8, HD), f32)
        for b in range(NB):
            rows = slice(b * PAGE, (b + 1) * PAGE)
            acc[h, b, 0] = dk[rows]
            acc[h, b, 1] = dv[rows]
            gk_terms += fold(dk[rows] * kvb[h, b, 0].astype(f32), jnp.sum)
        remote(
            acc.at[h, pl.ds(theirs, NZ)], sib.at[h], sl_s.at[h], sl_r.at[h], sibling
        ).start()
        dx, own_terms = norm_grad(kc[:, cols(h)].astype(f32), kg[...], dk[PL:])
        dkc[:, cols(h)] = dx.astype(bf16)
        dvc[:, cols(h)] = dv[PL:].astype(bf16)
        gk[...] += gk_terms / kg[...] + fold(own_terms, jnp.sum)
        kt = jnp.concatenate([keys(t).T for t in range(NT_)], axis=1)
        dqt = dot(kt, ds[...], NN)
        gq_terms = jnp.zeros((8, HD), f32)
        for g in range(GRP):
            dy = dqt[:, g * SLOTS : (g + 1) * SLOTS].T * SCALE
            at = cols(h, g, GRP)
            dx, terms = norm_grad(qv[:, at].astype(f32), qg[...], dy)
            gq_terms += fold(terms, jnp.sum)
            dqv[:, at] = dx.astype(bf16)
        gq[...] += gq_terms
        span = pl.ds(pl.multiple_of(h * ROWS, ROWS), ROWS)
        pltpu.make_async_copy(dqv.at[:, span], dq_hbm.at[:, span], dq_sem.at[h]).start()

    def hop(h, d, j):
        return remote(
            rss.at[h, d, j], rsr.at[h, d, j], rs_s.at[h, d, j], rs_r.at[h, d, j], zdev(z + 1 - 2 * d)
        )

    def chip_sum(h, t):
        return acc[h, c * NZ + t] + sib[h, t]

    def reduce(tick):
        for j in (1, 2, 3):
            h = tick - FILL - j

            @pl.when(between(h, 0, KVH))
            def _(h=h, j=j):
                odd = lax.rem(h, 2)
                if j == 1:
                    remote(sib.at[h], sib.at[h], sl_s.at[h], sl_r.at[h], sibling).wait_recv()
                for d in (0, 1):
                    length = 3 + (odd if d else 1 - odd)
                    val = chip_sum(h, zmod(z + (1 - 2 * d) * (length - j + 1)))
                    if j > 1:
                        hop(h, d, j - 2).wait_recv()
                        val = val + rsr[h, d, j - 2].astype(f32)
                    rss[h, d, j - 1] = val.astype(bf16)
                    hop(h, d, j - 1).start()

        h = tick - FILL - 4

        @pl.when(between(h, 0, KVH))
        def _():
            d = lax.rem(h, 2)
            hop(h, d, 2).wait_recv()
            val = chip_sum(h, zmod(z + 1 - 2 * d)) + rsr[h, d, 2].astype(f32)
            rss[h, d, 3] = val.astype(bf16)
            hop(h, d, 3).start()

        hf = tick - FILL - 5

        @pl.when(between(hf, 0, KVH))
        def _():
            d = lax.rem(hf, 2)
            hop(hf, d, 3).wait_recv()
            hop(hf, 1 - d, 2).wait_recv()
            val = chip_sum(hf, z) + (rsr[hf, d, 3].astype(f32) + rsr[hf, 1 - d, 2].astype(f32))
            dx, _ = norm_grad(kp[:, cols(hf)].astype(f32), kg[...], val[0])
            dkp[:, cols(hf)] = dx.astype(bf16)
            dvp[:, cols(hf)] = val[1].astype(bf16)

    base = (0, 2, 10, 14)

    def gain_copy(i, slot_of, src_dev, n):
        return remote(gsend.at[i], grecv.at[slot_of], g_s.at[i, n], g_r.at[slot_of], src_dev)

    def share_gains(i):
        index = stages[i][0][1]
        slot = base[i] + index
        grecv[slot] = gsend[i]
        for n, (_, _, dev) in enumerate(stages[i]):
            gain_copy(i, slot, dev, n).start()

    def sum_gains(i):
        index = stages[i][0][1]
        size = (2, 8, 4, 4)[i]
        for n in range(1, size):
            slot = base[i] + lax.rem(index + n, size)
            gain_copy(i, slot, stages[i][0][2], 0).wait_recv()
        total = grecv[base[i]]
        for n in range(1, size):
            total = total + grecv[base[i] + n]
        return total

    def step(tick, carry):
        gather(tick)
        reduce(tick)

        for i in range(4):

            @pl.when(tick == FILL + KVH + i)
            def _(i=i):
                if i == 0:
                    q_sum = jnp.sum(gq[...], axis=0, keepdims=True)
                    k_sum = jnp.sum(gk[...], axis=0, keepdims=True)
                    row = lax.broadcasted_iota(jnp.int32, (8, HD), 0)
                    gsend[0] = jnp.where(row == 0, q_sum, jnp.where(row == 1, k_sum, 0.0))
                else:
                    gsend[i] = sum_gains(i - 1)
                share_gains(i)

        @pl.when(tick < 4)
        def _():
            part = pl.ds(pl.multiple_of(tick * quarter, quarter), quarter)
            pltpu.make_async_copy(q_hbm.at[:, part], qv.at[:, part], q_sem.at[tick]).wait()
            prepare(2 * tick)
            prepare(2 * tick + 1)

        @pl.when(tick == 4)
        def _():
            pltpu.make_async_copy(do_hbm, dov, do_sem).wait()

        @pl.when(between(tick, FILL, FILL + KVH))
        def _():
            compute(tick - FILL)

        return carry

    lax.fori_loop(0, TICKS, step, 0)
    gains[...] = sum_gains(3)

    def drain(h, carry):
        odd = lax.rem(h, 2)
        for d in (0, 1):
            for k in range(3):
                block(h, mine, ag_s.at[h, d, k], ag_r.at[h, mine], sibling).wait_send()
                hop(h, d, k).wait_send()
        block(h, mine, ag_s.at[h, odd, 3], ag_r.at[h, mine], sibling).wait_send()
        hop(h, odd, 3).wait_send()
        for k in range(NZ):
            block(h, mine, ag_b.at[h, k], ag_r.at[h, mine], sibling).wait_send()
        remote(sib.at[h], sib.at[h], sl_s.at[h], sl_r.at[h], sibling).wait_send()
        span = pl.ds(pl.multiple_of(h * ROWS, ROWS), ROWS)
        pltpu.make_async_copy(dqv.at[:, span], dq_hbm.at[:, span], dq_sem.at[h]).wait()
        return carry

    lax.fori_loop(0, KVH, drain, 0)
    for i in range(4):
        for n, (_, _, dev) in enumerate(stages[i]):
            gain_copy(i, base[i], dev, n).wait_send()


def body(q_raw, d_out, k_prompt, v_prompt, k_comp, v_comp, lengths, q_gain, k_gain):
    vmem = pl.BlockSpec(memory_space=pltpu.VMEM)
    hbm = pl.BlockSpec(memory_space=pl.ANY)
    dma = pltpu.SemaphoreType.DMA
    wide = KVH * HD
    shape = jax.ShapeDtypeStruct
    outs = pl.pallas_call(
        kernel,
        out_shape=(
            shape((SLOTS, GRP * wide), bf16),
            shape((SLOTS, wide), bf16),
            shape((SLOTS, wide), bf16),
            shape((PAGE, wide), bf16),
            shape((PAGE, wide), bf16),
            shape((8, HD), f32),
        ),
        in_specs=[hbm, hbm] + [vmem] * 7,
        out_specs=[hbm] + [vmem] * 5,
        scratch_shapes=[
            pltpu.VMEM((SLOTS, GRP * wide), bf16),
            pltpu.VMEM((SLOTS, GRP * wide), bf16),
            pltpu.VMEM((SLOTS, GRP * wide), bf16),
            pltpu.VMEM((KVH, ROWS, HD), bf16),
            pltpu.VMEM((KVH, SLOTS, HD), bf16),
            pltpu.VMEM((SLOTS, CH), f32),
            pltpu.VMEM((KVH, NB, 2, PAGE, HD), bf16),
            pltpu.VMEM((KEYS, ROWS), f32),
            pltpu.VMEM((KEYS, ROWS), f32),
            pltpu.VMEM((KEYS, ROWS), bf16),
            pltpu.VMEM((KEYS, ROWS), bf16),
            pltpu.VMEM((KVH, NB, 2, PAGE, HD), f32),
            pltpu.VMEM((KVH, NZ, 2, PAGE, HD), f32),
            pltpu.VMEM((KVH, 2, 4, 2, PAGE, HD), bf16),
            pltpu.VMEM((KVH, 2, 4, 2, PAGE, HD), bf16),
            pltpu.VMEM((8, HD), f32),
            pltpu.VMEM((8, HD), f32),
            pltpu.VMEM((4, 8, HD), f32),
            pltpu.VMEM((18, 8, HD), f32),
            dma((4,)),
            dma(()),
            dma((KVH,)),
            dma((KVH, 2, 4)),
            dma((KVH, 8)),
            dma((KVH, NB)),
            dma((KVH,)),
            dma((KVH,)),
            dma((KVH, 2, 4)),
            dma((KVH, 2, 4)),
            dma((4, 8)),
            dma((18,)),
        ],
        compiler_params=pltpu.CompilerParams(
            collective_id=0, has_side_effects=True, vmem_limit_bytes=58 * 2**20
        ),
        cost_estimate=pl.CostEstimate(flops=13 * 10**9, bytes_accessed=8 * 2**20, transcendentals=10**7),
        name="attention_backward",
    )(
        q_raw[0], d_out[0], k_prompt[0], v_prompt[0], k_comp[0], v_comp[0], lengths[0],
        q_gain.reshape(1, HD), k_gain.reshape(1, HD),
    )
    dq, dk_own, dv_own, dk_page, dv_page, gains = outs
    return dq[None], dk_own[None], dv_own[None], dk_page[None], dv_page[None], gains[0], gains[1]


def solution(mesh):
    split = P("prompt", "comp", None)
    return jax.shard_map(
        body,
        mesh=mesh,
        in_specs=(split,) * 7 + (P(), P()),
        out_specs=(split,) * 5 + (P(), P()),
        check_vma=False,
    )
```

```python
import functools
import math

import jax
import jax.numpy as jnp
from jax import lax
from jax.experimental import pallas as pl
from jax.experimental.pallas import tpu as pltpu
from jax.sharding import PartitionSpec as P

MESH = pl.DeviceIdType.MESH
f32 = jnp.float32
bf16 = jnp.bfloat16
KVH = 8
GRP = 8
HD = 128
SLOTS = 128
PL = 1024
KEYS = PL + SLOTS
ROWS = GRP * SLOTS
PAGE = 64
NZ = 8
NB = 16
CH = 256
TILE = 128
NT_ = KEYS // TILE
EPS = 1e-6
SCALE = 1.0 / math.sqrt(HD)
LOG2 = SCALE * math.log2(math.e)
HALF = ROWS // 2

NT = (((1,), (1,)), ((), ()))
NN = (((1,), (0,)), ((), ()))


def dot(a, b, dims):
    return lax.dot_general(a, b, dims, preferred_element_type=f32)


def fold(x, op):
    return op(x.reshape(x.shape[0] // 8, 8, x.shape[1]), axis=0)


def cols(h, i=0, n=1):
    return pl.ds(pl.multiple_of(h * (n * HD) + i * HD, HD), HD)


def inv_rms(x):
    return lax.rsqrt(jnp.mean(x * x, axis=-1, keepdims=True) + EPS)


def norm_grad(x, gain, dy):
    r = inv_rms(x)
    xr = x * r
    u = dy * gain
    dx = r * (u - xr * jnp.mean(xr * u, axis=-1, keepdims=True))
    return dx, dy * xr


def remote(src, dst, send, recv, device):
    return pltpu.make_async_remote_copy(
        src_ref=src, dst_ref=dst, send_sem=send, recv_sem=recv, device_id=device, device_id_type=MESH
    )


def kernel(
    q_hbm, do_hbm, kp, vp, kc, vc, lens, qg, kg,
    dq_hbm, dkc, dvc, dkp, dvp, gq_out, gk_out,
    qv, dov, qn, okn, vis, kvb, sc, dp, pb, ds, pdv, pdk, acc, sib, rsr, rss, gq, gk, gsend, grecv,
    q_sem, do_sem, dq_sem, ag_s, ag_b, ag_r, ag_v, sl_s, sl_r, rs_s, rs_r, g_s, g_r,
):
    p = lax.axis_index("prompt")
    me = lax.axis_index("comp")
    z, c = me // 2, me % 2
    px, py = p // 4, p % 4
    zmod = lambda v: lax.rem(v + 2 * NZ, NZ)
    zdev = lambda v: {"comp": zmod(v) * 2 + c}
    sibling = {"comp": z * 2 + (1 - c)}
    mine = c * NZ + z
    theirs = (1 - c) * NZ
    stages = (
        [(1, c, sibling)],
        [(8, z, zdev(z + i)) for i in range(1, 8)],
        [(4, px, {"prompt": lax.rem(px + i, 4) * 4 + py}) for i in range(1, 4)],
        [(4, py, {"prompt": px * 4 + lax.rem(py + i, 4)}) for i in range(1, 4)],
    )

    barrier = pltpu.get_barrier_semaphore()
    for stage in stages:
        for _, _, dev in stage:
            pl.semaphore_signal(barrier, inc=1, device_id=dev, device_id_type=MESH)

    quarter = ROWS * 2
    for i in range(4):
        part = pl.ds(i * quarter, quarter)
        pltpu.make_async_copy(q_hbm.at[:, part], qv.at[:, part], q_sem.at[i]).start()
    pltpu.make_async_copy(do_hbm, dov, do_sem).start()

    for h in range(KVH):
        x = kp[:, h * HD : (h + 1) * HD].astype(f32)
        kvb[h, mine, 0] = (x * inv_rms(x) * kg[...]).astype(bf16)
        kvb[h, mine, 1] = vp[:, h * HD : (h + 1) * HD]
        x = kc[:, h * HD : (h + 1) * HD].astype(f32)
        okn[h] = (x * inv_rms(x) * kg[...]).astype(bf16)
    gq[...] = jnp.zeros_like(gq)
    gk[...] = jnp.zeros_like(gk)
    t_at = lax.broadcasted_iota(jnp.int32, (SLOTS, SLOTS), 0)
    s_at = lax.broadcasted_iota(jnp.int32, (SLOTS, SLOTS), 1)
    seg_t = jnp.zeros((SLOTS, SLOTS), jnp.int32)
    seg_s = jnp.zeros((SLOTS, SLOTS), jnp.int32)
    end = jnp.zeros((1, 1), jnp.int32)
    for i in range(4):
        end = end + lens[0:1, i : i + 1]
        seg_t += (t_at >= end).astype(jnp.int32)
        seg_s += (s_at >= end).astype(jnp.int32)
    seen = ((seg_t == seg_s) & (t_at <= s_at)).astype(f32)
    vis[...] = jnp.concatenate([seen] * (CH // SLOTS), axis=1)

    pl.semaphore_wait(barrier, sum(len(s) for s in stages))

    def between(v, lo, hi):
        return jnp.logical_and(v >= lo, v < hi)

    def block(h, slot, send, recv_slot_sem, dev):
        return remote(kvb.at[h, slot], kvb.at[h, slot], send, recv_slot_sem, dev)

    def arrived(h, slot):
        block(h, slot, ag_b.at[h, 0], ag_r.at[h, slot], sibling).wait_recv()

    def half_block(h, slot, n, send, recv, dev):
        return remote(kvb.at[h, slot, n], kvb.at[h, slot, n], send, recv, dev)

    def forward(h, slot, n):
        block(h, slot, ag_b.at[h, n], ag_r.at[h, slot], sibling).start()

    def gather_near(h):
        @pl.when(between(h, 0, KVH))
        def _():
            for n, i in enumerate((2, -2, 1, -1)):
                block(h, mine, ag_s.at[h, n], ag_r.at[h, mine], zdev(z + i)).start()
            forward(h, mine, 0)

    def gather_far(h):
        @pl.when(between(h, 0, KVH))
        def _():
            for n, step in enumerate((1, -1)):
                slot = c * NZ + zmod(z - 2 * step)
                arrived(h, slot)
                block(h, slot, ag_s.at[h, 4 + n], ag_r.at[h, slot], zdev(z + step)).start()
                recv = ag_v.at[h] if n else ag_r.at[h, slot]
                half_block(h, slot, n, ag_s.at[h, 6 + n], recv, zdev(z + 2 * step)).start()
                forward(h, slot, 1 + n)
            for n, step in enumerate((1, -1)):
                slot = c * NZ + zmod(z - step)
                arrived(h, slot)
                forward(h, slot, 3 + n)

    def gather_end(h, low):
        @pl.when(between(h, low, KVH))
        def _():
            for n, step in enumerate((1, -1)):
                slot = c * NZ + zmod(z - 3 * step)
                arrived(h, slot)
                forward(h, slot, 5 + n)
            slot = c * NZ + zmod(z + 4)
            half_block(h, slot, 0, ag_s.at[h, 6], ag_r.at[h, slot], sibling).wait_recv()
            half_block(h, slot, 1, ag_s.at[h, 7], ag_v.at[h], sibling).wait_recv()
            forward(h, slot, 7)

    def prepare(h):
        for g in range(GRP):
            x = qv[:, cols(h, g, GRP)].astype(f32)
            y = x * inv_rms(x) * qg[...]
            near = y.astype(bf16)
            at = slice(g * SLOTS, (g + 1) * SLOTS)
            qn[h, at, :HD] = near
            qn[h, at, HD:] = (y - near.astype(f32)).astype(bf16)

    def keys(h, t):
        return okn[h] if t == NT_ - 1 else kvb[h, 2 * t : 2 * t + 2, 0].reshape(TILE, HD)

    def vals(h, t):
        return vc[:, cols(h)] if t == NT_ - 1 else kvb[h, 2 * t : 2 * t + 2, 1].reshape(TILE, HD)

    def soft(h, half):
        heads = range(half * GRP // 2, (half + 1) * GRP // 2)
        grads = jnp.concatenate([dov[:, cols(h, g, GRP)] for g in heads], axis=0)
        for n, lo in enumerate(range(half * HALF, (half + 1) * HALF, CH)):
            at = slice(lo, lo + CH)
            own = slice(lo - half * HALF, lo - half * HALF + CH)
            qc = qn[h, at, :HD]
            gc = grads[own]
            top = None
            for t in range(NT_):
                ts = slice(t * TILE, (t + 1) * TILE)
                s = dot(keys(h, t), qc, NT)
                if t == NT_ - 1:
                    s = jnp.where(vis[...] > 0, s, -1e30)
                sc[n, ts] = s
                part = fold(s, jnp.max)
                top = part if top is None else jnp.maximum(top, part)
            top = jnp.max(top, axis=0, keepdims=True) * LOG2
            total = None
            for t in range(NT_):
                ts = slice(t * TILE, (t + 1) * TILE)
                e = jnp.exp2(sc[n, ts] * LOG2 - top)
                sc[n, ts] = e
                part = fold(e, jnp.sum)
                total = part if total is None else total + part
            inv = 1.0 / jnp.sum(total, axis=0, keepdims=True)
            delta = None
            for t in range(NT_):
                ts = slice(t * TILE, (t + 1) * TILE)
                d = dot(vals(h, t), gc, NT)
                dp[n, ts] = d
                b = (sc[n, ts] * inv).astype(bf16)
                pb[ts, own] = b
                part = fold(b.astype(f32) * d, jnp.sum)
                delta = part if delta is None else delta + part
            delta = jnp.sum(delta, axis=0, keepdims=True)
            for t in range(NT_):
                ts = slice(t * TILE, (t + 1) * TILE)
                ds[h, ts, at] = (sc[n, ts] * inv * (dp[n, ts] - delta)).astype(bf16)
        at = slice(half * HALF, (half + 1) * HALF)
        return dot(pb[...], grads, NN), dot(ds[h, :, at], qn[h, at], NN)

    def compute(h, between_halves):
        for i in range(NZ):
            arrived(h, theirs + i)
        dv, dk = soft(h, 0)
        pdv[...] = dv
        pdk[...] = dk
        between_halves()
        dv, dk = soft(h, 1)
        dv = dv + pdv[...]
        both = (dk + pdk[...]) * SCALE
        dk = both[:, :HD]
        exact = dk + both[:, HD:]
        gk_terms = jnp.zeros((8, HD), f32)
        gq_terms = fold(exact[PL:] * okn[h].astype(f32), jnp.sum)
        for b in range(NB):
            rows = slice(b * PAGE, (b + 1) * PAGE)
            acc[h, b, 0] = dk[rows]
            acc[h, b, 1] = dv[rows]
            key = kvb[h, b, 0].astype(f32)
            gk_terms += fold(dk[rows] * key, jnp.sum)
            gq_terms += fold(exact[rows] * key, jnp.sum)
        remote(
            acc.at[h, pl.ds(theirs, NZ)], sib.at[h], sl_s.at[h], sl_r.at[h], sibling
        ).start()
        dx, own_terms = norm_grad(kc[:, cols(h)].astype(f32), kg[...], dk[PL:])
        dkc[:, cols(h)] = dx.astype(bf16)
        dvc[:, cols(h)] = dv[PL:].astype(bf16)
        gk[...] += gk_terms / kg[...] + fold(own_terms, jnp.sum)
        gq[...] += gq_terms / qg[...]

    def queries(h):
        kt = jnp.concatenate([keys(h, t).T for t in range(NT_)], axis=1)
        dqt = dot(kt, ds[h], NN)
        for g in range(GRP):
            dy = dqt[:, g * SLOTS : (g + 1) * SLOTS].T * SCALE
            at = cols(h, g, GRP)
            dx, _ = norm_grad(qv[:, at].astype(f32), qg[...], dy)
            qv[:, at] = dx.astype(bf16)
        dq_copy(h).start()

    def dq_copy(h):
        span = pl.ds(pl.multiple_of(h * ROWS, ROWS), ROWS)
        return pltpu.make_async_copy(qv.at[:, span], dq_hbm.at[:, span], dq_sem.at[h])

    def hop(h, d, j):
        return remote(
            rss.at[h, d, j], rsr.at[h, d, j], rs_s.at[h, d, j], rs_r.at[h, d, j], zdev(z + 1 - 2 * d)
        )

    def chip_sum(h, t):
        return acc[h, c * NZ + t] + sib[h, t]

    def reduce_hop(h, j):
        @pl.when(between(h, 0, KVH))
        def _():
            odd = lax.rem(h, 2)
            if j == 4:
                hop(h, odd, 2).wait_recv()
                val = chip_sum(h, zmod(z + 1 - 2 * odd)) + rsr[h, odd, 2].astype(f32)
                rss[h, odd, 3] = val.astype(bf16)
                hop(h, odd, 3).start()
                return
            if j == 1:
                remote(sib.at[h], sib.at[h], sl_s.at[h], sl_r.at[h], sibling).wait_recv()
            for d in (0, 1):
                length = 3 + (odd if d else 1 - odd)
                val = chip_sum(h, zmod(z + (1 - 2 * d) * (length - j + 1)))
                if j > 1:
                    hop(h, d, j - 2).wait_recv()
                    val = val + rsr[h, d, j - 2].astype(f32)
                rss[h, d, j - 1] = val.astype(bf16)
                hop(h, d, j - 1).start()

    def reduce_end(h):
        @pl.when(between(h, 0, KVH))
        def _():
            d = lax.rem(h, 2)
            hop(h, d, 3).wait_recv()
            hop(h, 1 - d, 2).wait_recv()
            val = chip_sum(h, z) + (rsr[h, d, 3].astype(f32) + rsr[h, 1 - d, 2].astype(f32))
            dx, _ = norm_grad(kp[:, cols(h)].astype(f32), kg[...], val[0])
            dkp[:, cols(h)] = dx.astype(bf16)
            dvp[:, cols(h)] = val[1].astype(bf16)

    def reduce(i):
        for j in (4, 3, 2, 1):
            reduce_hop(i - j, j)
        reduce_end(i - 5)

    base = (0, 2, 10, 14)

    def gain_copy(i, slot_of, src_dev, n):
        return remote(gsend.at[i], grecv.at[slot_of], g_s.at[i, n], g_r.at[slot_of], src_dev)

    def share_gains(i):
        index = stages[i][0][1]
        slot = base[i] + index
        grecv[slot] = gsend[i]
        for n, (_, _, dev) in enumerate(stages[i]):
            gain_copy(i, slot, dev, n).start()

    def sum_gains(i):
        index = stages[i][0][1]
        size = (2, 8, 4, 4)[i]
        for n in range(1, size):
            slot = base[i] + lax.rem(index + n, size)
            gain_copy(i, slot, stages[i][0][2], 0).wait_recv()
        total = grecv[base[i]]
        for n in range(1, size):
            total = total + grecv[base[i] + n]
        return total

    gather_near(0)
    gather_near(1)

    def fill(n, carry):
        part = pl.ds(pl.multiple_of(n * quarter, quarter), quarter)
        pltpu.make_async_copy(q_hbm.at[:, part], qv.at[:, part], q_sem.at[n]).wait()
        prepare(2 * n)
        prepare(2 * n + 1)

        @pl.when(n >= 2)
        def _():
            gather_far(n - 2)

        return carry

    lax.fori_loop(0, 4, fill, 0)
    gather_near(2)
    pltpu.make_async_copy(do_hbm, dov, do_sem).wait()
    gather_end(0, 0)

    def main(i, carry):
        gather_end(i + 1, 2)
        gather_far(i + 2)
        gather_near(i + 3)

        def between_halves():
            @pl.when(i == 0)
            def _():
                gather_end(1, 1)

            reduce(i)

        compute(i, between_halves)
        return carry

    lax.fori_loop(0, KVH, main, 0)

    def gain_step(i):
        if i == 0:
            q_sum = jnp.sum(gq[...], axis=0, keepdims=True)
            k_sum = jnp.sum(gk[...], axis=0, keepdims=True)
            row = lax.broadcasted_iota(jnp.int32, (8, HD), 0)
            gsend[0] = jnp.where(row == 0, q_sum, jnp.where(row == 1, k_sum, 0.0))
        else:
            gsend[i] = sum_gains(i - 1)
        share_gains(i)

    def late(n, carry):
        for i in range(4):

            @pl.when(n == i)
            def _(i=i):
                gain_step(i)

        @pl.when(n < 4)
        def _():
            queries(2 * n)

        reduce(KVH + n)

        @pl.when(n < 4)
        def _():
            queries(2 * n + 1)

        return carry

    lax.fori_loop(0, 5, late, 0)
    total = sum_gains(3)
    gq_out[...] = total[0:1]
    gk_out[...] = total[1:2]

    def drain(h, carry):
        odd = lax.rem(h, 2)
        for d in (0, 1):
            for k in range(3):
                hop(h, d, k).wait_send()
        hop(h, odd, 3).wait_send()

        for k in range(6):
            block(h, mine, ag_s.at[h, k], ag_r.at[h, mine], sibling).wait_send()
        for k in (0, 1):
            half_block(h, mine, k, ag_s.at[h, 6 + k], ag_v.at[h], sibling).wait_send()
        for k in range(NZ):
            block(h, mine, ag_b.at[h, k], ag_r.at[h, mine], sibling).wait_send()
        remote(sib.at[h], sib.at[h], sl_s.at[h], sl_r.at[h], sibling).wait_send()
        dq_copy(h).wait()
        return carry

    lax.fori_loop(0, KVH, drain, 0)
    for i in range(4):
        for n, (_, _, dev) in enumerate(stages[i]):
            gain_copy(i, base[i], dev, n).wait_send()


def body(q_raw, d_out, k_prompt, v_prompt, k_comp, v_comp, lengths, q_gain, k_gain):
    vmem = pl.BlockSpec(memory_space=pltpu.VMEM)
    hbm = pl.BlockSpec(memory_space=pl.ANY)
    dma = pltpu.SemaphoreType.DMA
    wide = KVH * HD
    shape = jax.ShapeDtypeStruct
    outs = pl.pallas_call(
        kernel,
        out_shape=(
            shape((SLOTS, GRP * wide), bf16),
            shape((SLOTS, wide), bf16),
            shape((SLOTS, wide), bf16),
            shape((PAGE, wide), bf16),
            shape((PAGE, wide), bf16),
            shape((1, HD), f32),
            shape((1, HD), f32),
        ),
        in_specs=[hbm, hbm] + [vmem] * 7,
        out_specs=[hbm] + [vmem] * 6,
        scratch_shapes=[
            pltpu.VMEM((SLOTS, GRP * wide), bf16),
            pltpu.VMEM((SLOTS, GRP * wide), bf16),
            pltpu.VMEM((KVH, ROWS, 2 * HD), bf16),
            pltpu.VMEM((KVH, SLOTS, HD), bf16),
            pltpu.VMEM((SLOTS, CH), f32),
            pltpu.VMEM((KVH, NB, 2, PAGE, HD), bf16),
            pltpu.VMEM((2, KEYS, CH), f32),
            pltpu.VMEM((2, KEYS, CH), f32),
            pltpu.VMEM((KEYS, HALF), bf16),
            pltpu.VMEM((KVH, KEYS, ROWS), bf16),
            pltpu.VMEM((KEYS, HD), f32),
            pltpu.VMEM((KEYS, 2 * HD), f32),
            pltpu.VMEM((KVH, NB, 2, PAGE, HD), f32),
            pltpu.VMEM((KVH, NZ, 2, PAGE, HD), f32),
            pltpu.VMEM((KVH, 2, 4, 2, PAGE, HD), bf16),
            pltpu.VMEM((KVH, 2, 4, 2, PAGE, HD), bf16),
            pltpu.VMEM((8, HD), f32),
            pltpu.VMEM((8, HD), f32),
            pltpu.VMEM((4, 8, HD), f32),
            pltpu.VMEM((18, 8, HD), f32),
            dma((4,)),
            dma(()),
            dma((KVH,)),
            dma((KVH, 8)),
            dma((KVH, 8)),
            dma((KVH, NB)),
            dma((KVH,)),
            dma((KVH,)),
            dma((KVH,)),
            dma((KVH, 2, 4)),
            dma((KVH, 2, 4)),
            dma((4, 8)),
            dma((18,)),
        ],
        compiler_params=pltpu.CompilerParams(
            collective_id=0, has_side_effects=True, vmem_limit_bytes=60 * 2**20
        ),
        cost_estimate=pl.CostEstimate(flops=13 * 10**9, bytes_accessed=8 * 2**20, transcendentals=10**7),
        name="attention_backward",
    )(
        q_raw[0], d_out[0], k_prompt[0], v_prompt[0], k_comp[0], v_comp[0], lengths[0],
        q_gain.reshape(1, HD), k_gain.reshape(1, HD),
    )
    *large, gq, gk = finish(outs)
    return tuple(x[None] for x in large) + (gq.reshape(HD), gk.reshape(HD))


def finish_kernel(*refs):
    ins, outs, stage, sem_in, sem_out = refs[:7], refs[7:14], refs[14:19], refs[19], refs[20]
    pieces = [(0, pl.ds(i * (SLOTS // 4), SLOTS // 4)) for i in range(4)]
    pieces += [(i, pl.ds(0, ins[i].shape[0])) for i in range(1, 5)]
    loads = [pltpu.make_async_copy(ins[i].at[at], stage[i].at[at], sem_in.at[n]) for n, (i, at) in enumerate(pieces)]
    stores = [pltpu.make_async_copy(stage[i].at[at], outs[i].at[at], sem_out.at[n]) for n, (i, at) in enumerate(pieces)]
    for copy in loads:
        copy.start()
    outs[5][...] = ins[5][...]
    outs[6][...] = ins[6][...]
    for load, store in zip(loads, stores):
        load.wait()
        store.start()
    for copy in stores:
        copy.wait()


def finish(arrays):
    vmem = pl.BlockSpec(memory_space=pltpu.VMEM)
    hbm = pl.BlockSpec(memory_space=pl.ANY)
    return pl.pallas_call(
        finish_kernel,
        out_shape=[jax.ShapeDtypeStruct(x.shape, x.dtype) for x in arrays],
        in_specs=[hbm] * 5 + [vmem] * 2,
        out_specs=[hbm] * 5 + [vmem] * 2,
        scratch_shapes=[pltpu.VMEM(x.shape, x.dtype) for x in arrays[:5]]
        + [pltpu.SemaphoreType.DMA((8,)), pltpu.SemaphoreType.DMA((8,))],
        name="finish",
    )(*arrays)


def solution(mesh):
    split = P("prompt", "comp", None)
    return jax.shard_map(
        body,
        mesh=mesh,
        in_specs=(split,) * 7 + (P(), P()),
        out_specs=(split,) * 5 + (P(), P()),
        check_vma=False,
    )
```

```python
import functools
import math

import jax
import jax.numpy as jnp
from jax import lax
from jax.experimental import pallas as pl
from jax.experimental.pallas import tpu as pltpu
from jax.sharding import PartitionSpec as P

MESH = pl.DeviceIdType.MESH
f32 = jnp.float32
bf16 = jnp.bfloat16
KVH = 8
GRP = 8
HD = 128
SLOTS = 128
PL = 1024
KEYS = PL + SLOTS
ROWS = GRP * SLOTS
PAGE = 64
NZ = 8
NB = 16
CH = 256
TILE = 128
NT_ = KEYS // TILE
EPS = 1e-6
SCALE = 1.0 / math.sqrt(HD)
LOG2 = SCALE * math.log2(math.e)
HALF = ROWS // 2
EARLY = 3

NT = (((1,), (1,)), ((), ()))
NN = (((1,), (0,)), ((), ()))


def dot(a, b, dims):
    return lax.dot_general(a, b, dims, preferred_element_type=f32)


def fold(x, op):
    return op(x.reshape(x.shape[0] // 8, 8, x.shape[1]), axis=0)


def cols(h, i=0, n=1):
    return pl.ds(pl.multiple_of(h * (n * HD) + i * HD, HD), HD)


def inv_rms(x):
    return lax.rsqrt(jnp.mean(x * x, axis=-1, keepdims=True) + EPS)


def norm_grad(x, gain, dy):
    r = inv_rms(x)
    xr = x * r
    u = dy * gain
    dx = r * (u - xr * jnp.mean(xr * u, axis=-1, keepdims=True))
    return dx, dy * xr


def remote(src, dst, send, recv, device):
    return pltpu.make_async_remote_copy(
        src_ref=src, dst_ref=dst, send_sem=send, recv_sem=recv, device_id=device, device_id_type=MESH
    )


def kernel(
    q_hbm, do_hbm, kp, vp, kc, vc, lens, qg, kg,
    dq_hbm, dkc, dvc, dkp, dvp, gq_out, gk_out,
    qv, dov, qn, okn, qgt, vis, kvb, sc, dp, pb, ds, pdv, pdk, acc, slab, sib, rsr, rss, gq, gk, gsend, grecv,
    q_sem, do_sem, dq_sem, ag_s, ag_b, ag_r, ag_v, sl_s, sl_r, rs_s, rs_r, g_s, g_r,
):
    p = lax.axis_index("prompt")
    me = lax.axis_index("comp")
    z, c = me // 2, me % 2
    px, py = p // 4, p % 4
    zmod = lambda v: lax.rem(v + 2 * NZ, NZ)
    zdev = lambda v: {"comp": zmod(v) * 2 + c}
    sibling = {"comp": z * 2 + (1 - c)}
    mine = c * NZ + z
    theirs = (1 - c) * NZ
    stages = (
        [(1, c, sibling)],
        [(8, z, zdev(z + i)) for i in range(1, 8)],
        [(4, px, {"prompt": lax.rem(px + i, 4) * 4 + py}) for i in range(1, 4)],
        [(4, py, {"prompt": px * 4 + lax.rem(py + i, 4)}) for i in range(1, 4)],
    )

    barrier = pltpu.get_barrier_semaphore()
    for stage in stages:
        for _, _, dev in stage:
            pl.semaphore_signal(barrier, inc=1, device_id=dev, device_id_type=MESH)

    quarter = ROWS * 2
    for i in range(4):
        part = pl.ds(i * quarter, quarter)
        pltpu.make_async_copy(q_hbm.at[:, part], qv.at[:, part], q_sem.at[i]).start()
    pltpu.make_async_copy(do_hbm, dov, do_sem).start()

    for h in range(KVH):
        x = kp[:, h * HD : (h + 1) * HD].astype(f32)
        kvb[h, mine, 0] = (x * inv_rms(x) * kg[...]).astype(bf16)
        kvb[h, mine, 1] = vp[:, h * HD : (h + 1) * HD]
        x = kc[:, h * HD : (h + 1) * HD].astype(f32)
        okn[h] = (x * inv_rms(x) * kg[...]).astype(bf16)
    qgt[...] = jnp.broadcast_to(qg[...] * SCALE, (SLOTS, HD)).T
    gq[...] = jnp.zeros_like(gq)
    gk[...] = jnp.zeros_like(gk)
    t_at = lax.broadcasted_iota(jnp.int32, (SLOTS, SLOTS), 0)
    s_at = lax.broadcasted_iota(jnp.int32, (SLOTS, SLOTS), 1)
    seg_t = jnp.zeros((SLOTS, SLOTS), jnp.int32)
    seg_s = jnp.zeros((SLOTS, SLOTS), jnp.int32)
    end = jnp.zeros((1, 1), jnp.int32)
    for i in range(4):
        end = end + lens[0:1, i : i + 1]
        seg_t += (t_at >= end).astype(jnp.int32)
        seg_s += (s_at >= end).astype(jnp.int32)
    seen = ((seg_t == seg_s) & (t_at <= s_at)).astype(f32)
    vis[...] = jnp.concatenate([seen] * (CH // SLOTS), axis=1)

    pl.semaphore_wait(barrier, sum(len(s) for s in stages))

    def between(v, lo, hi):
        return jnp.logical_and(v >= lo, v < hi)

    def block(h, slot, send, recv_slot_sem, dev):
        return remote(kvb.at[h, slot], kvb.at[h, slot], send, recv_slot_sem, dev)

    def arrived(h, slot):
        block(h, slot, ag_b.at[h, 0], ag_r.at[h, slot], sibling).wait_recv()

    def half_block(h, slot, n, send, recv, dev):
        return remote(kvb.at[h, slot, n], kvb.at[h, slot, n], send, recv, dev)

    def forward(h, slot, n):
        block(h, slot, ag_b.at[h, n], ag_r.at[h, slot], sibling).start()

    def gather_near(h):
        @pl.when(between(h, 0, EARLY))
        def _():
            for n, i in enumerate((2, -2, 1, -1)):
                block(h, mine, ag_s.at[h, n], ag_r.at[h, mine], zdev(z + i)).start()
            forward(h, mine, 0)

    def gather_far(h):
        @pl.when(between(h, 0, EARLY))
        def _():
            for n, step in enumerate((1, -1)):
                slot = c * NZ + zmod(z - 2 * step)
                arrived(h, slot)
                block(h, slot, ag_s.at[h, 4 + n], ag_r.at[h, slot], zdev(z + step)).start()
                recv = ag_v.at[h] if n else ag_r.at[h, slot]
                half_block(h, slot, n, ag_s.at[h, 6 + n], recv, zdev(z + 2 * step)).start()
                forward(h, slot, 1 + n)
            for n, step in enumerate((1, -1)):
                slot = c * NZ + zmod(z - step)
                arrived(h, slot)
                forward(h, slot, 3 + n)

    def gather_end(h, low):
        @pl.when(between(h, low, EARLY))
        def _():
            for n, step in enumerate((1, -1)):
                slot = c * NZ + zmod(z - 3 * step)
                arrived(h, slot)
                forward(h, slot, 5 + n)
            slot = c * NZ + zmod(z + 4)
            half_block(h, slot, 0, ag_s.at[h, 6], ag_r.at[h, slot], sibling).wait_recv()
            half_block(h, slot, 1, ag_s.at[h, 7], ag_v.at[h], sibling).wait_recv()
            forward(h, slot, 7)

    def gather_hop(h, k):
        @pl.when(between(h, EARLY, KVH))
        def _():
            for d in (0, 1):
                step = 1 - 2 * d
                slot = c * NZ + zmod(z - step * k)
                if k:
                    arrived(h, slot)
                if k < 3:
                    block(h, slot, ag_s.at[h, 3 * d + k], ag_r.at[h, slot], zdev(z + step)).start()
                if k or not d:
                    forward(h, slot, 3 * d + k)
            if k == 3:
                step = 1 - 2 * lax.rem(h, 2)
                slot = c * NZ + zmod(z - step * 3)
                block(h, slot, ag_s.at[h, 6], ag_r.at[h, slot], zdev(z + step)).start()

    def gather_last(h):
        @pl.when(between(h, EARLY, KVH))
        def _():
            slot = c * NZ + zmod(z + 4)
            arrived(h, slot)
            forward(h, slot, 7)

    def prepare(h):
        for g in range(GRP):
            x = qv[:, cols(h, g, GRP)].astype(f32)
            y = x * inv_rms(x) * qg[...]
            near = y.astype(bf16)
            at = slice(g * SLOTS, (g + 1) * SLOTS)
            qn[h, at, :HD] = near
            qn[h, at, HD:] = (y - near.astype(f32)).astype(bf16)

    def keys(h, t):
        return okn[h] if t == NT_ - 1 else kvb[h, 2 * t : 2 * t + 2, 0].reshape(TILE, HD)

    def vals(h, t):
        return vc[:, cols(h)] if t == NT_ - 1 else kvb[h, 2 * t : 2 * t + 2, 1].reshape(TILE, HD)

    def soft(h, half):
        heads = range(half * GRP // 2, (half + 1) * GRP // 2)
        grads = jnp.concatenate([dov[:, cols(h, g, GRP)] for g in heads], axis=0)
        for n, lo in enumerate(range(half * HALF, (half + 1) * HALF, CH)):
            at = slice(lo, lo + CH)
            own = slice(lo - half * HALF, lo - half * HALF + CH)
            qc = qn[h, at, :HD]
            gc = grads[own]
            top = None
            for t in range(NT_):
                ts = slice(t * TILE, (t + 1) * TILE)
                s = dot(keys(h, t), qc, NT)
                if t == NT_ - 1:
                    s = jnp.where(vis[...] > 0, s, -1e30)
                sc[n, ts] = s
                part = fold(s, jnp.max)
                top = part if top is None else jnp.maximum(top, part)
            top = jnp.max(top, axis=0, keepdims=True) * LOG2
            total = None
            for t in range(NT_):
                ts = slice(t * TILE, (t + 1) * TILE)
                e = jnp.exp2(sc[n, ts] * LOG2 - top)
                sc[n, ts] = e
                part = fold(e, jnp.sum)
                total = part if total is None else total + part
            inv = 1.0 / jnp.sum(total, axis=0, keepdims=True)
            delta = None
            for t in range(NT_):
                ts = slice(t * TILE, (t + 1) * TILE)
                d = dot(vals(h, t), gc, NT)
                dp[n, ts] = d
                b = (sc[n, ts] * inv).astype(bf16)
                pb[ts, own] = b
                part = fold(b.astype(f32) * d, jnp.sum)
                delta = part if delta is None else delta + part
            delta = jnp.sum(delta, axis=0, keepdims=True)
            for t in range(NT_):
                ts = slice(t * TILE, (t + 1) * TILE)
                ds[h, ts, at] = (sc[n, ts] * inv * (dp[n, ts] - delta)).astype(bf16)
        at = slice(half * HALF, (half + 1) * HALF)
        return dot(pb[...], grads, NN), dot(ds[h, :, at], qn[h, at], NN)

    def compute(h, between_halves):
        for i in range(NZ):
            arrived(h, theirs + i)
        dv, dk = soft(h, 0)
        pdv[...] = dv
        pdk[...] = dk
        between_halves()
        dv, dk = soft(h, 1)
        dv = dv + pdv[...]
        both = (dk + pdk[...]) * SCALE
        dk = both[:, :HD]
        exact = dk + both[:, HD:]
        gk_terms = jnp.zeros((8, HD), f32)
        gq_terms = fold(exact[PL:] * okn[h].astype(f32), jnp.sum)
        for b in range(NB):
            rows = slice(b * PAGE, (b + 1) * PAGE)
            acc[h, b, 0] = dk[rows]
            acc[h, b, 1] = dv[rows]
            key = kvb[h, b, 0].astype(f32)
            gk_terms += fold(dk[rows] * key, jnp.sum)
            gq_terms += fold(exact[rows] * key, jnp.sum)
        slab[h] = acc[h, pl.ds(theirs, NZ)].astype(bf16)
        remote(slab.at[h], sib.at[h], sl_s.at[h], sl_r.at[h], sibling).start()
        dx, own_terms = norm_grad(kc[:, cols(h)].astype(f32), kg[...], dk[PL:])
        dkc[:, cols(h)] = dx.astype(bf16)
        dvc[:, cols(h)] = dv[PL:].astype(bf16)
        gk[...] += gk_terms / kg[...] + fold(own_terms, jnp.sum)
        gq[...] += gq_terms / qg[...]

    def queries(h):
        kt = jnp.concatenate([keys(h, t).T for t in range(NT_)], axis=1)
        dqt = dot(kt, ds[h], NN)
        for g in range(GRP):
            at = cols(h, g, GRP)
            x = qv[:, at].T.astype(f32)
            r = lax.rsqrt(jnp.mean(x * x, axis=0, keepdims=True) + EPS)
            xr = x * r
            u = dqt[:, g * SLOTS : (g + 1) * SLOTS] * qgt[...]
            dx = r * (u - xr * jnp.mean(xr * u, axis=0, keepdims=True))
            qv[:, at] = dx.astype(bf16).T
        dq_copy(h).start()

    def dq_copy(h):
        span = pl.ds(pl.multiple_of(h * ROWS, ROWS), ROWS)
        return pltpu.make_async_copy(qv.at[:, span], dq_hbm.at[:, span], dq_sem.at[h])

    def part(h, d, k):
        at = (h, d, k, d) if k == 3 else (h, d, k)
        reach = (1 - 2 * d) * (1 if k < 2 else 2)
        return remote(rss.at[at], rsr.at[at], rs_s.at[h, d, k], rs_r.at[h, d, k], zdev(z + reach))

    def chip_sum(h, t):
        return acc[h, c * NZ + t] + sib[h, t].astype(f32)

    def reduce_start(h):
        @pl.when(between(h, 0, KVH))
        def _():
            remote(sib.at[h], sib.at[h], sl_s.at[h], sl_r.at[h], sibling).wait_recv()
            for d, step in ((0, 1), (1, -1)):
                rss[h, d, 3, d] = chip_sum(h, zmod(z + 4))[d].astype(bf16)
                part(h, d, 3).start()
                rss[h, d, 0] = chip_sum(h, zmod(z + 3 * step)).astype(bf16)
                part(h, d, 0).start()
            for d, step in ((0, 1), (1, -1)):
                rss[h, d, 1] = chip_sum(h, zmod(z + step)).astype(bf16)
                part(h, d, 1).start()

    def reduce_mid(h):
        @pl.when(between(h, 0, KVH))
        def _():
            for d, step in ((0, 1), (1, -1)):
                part(h, d, 0).wait_recv()
                part(h, d, 3).wait_recv()
                val = chip_sum(h, zmod(z + 2 * step)) + rsr[h, d, 0].astype(f32)
                rss[h, d, 2, 1 - d] = val[1 - d].astype(bf16)
                rss[h, d, 2, d] = (val[d] + rsr[h, d, 3, d].astype(f32)).astype(bf16)
                part(h, d, 2).start()

    def reduce_end(h):
        @pl.when(between(h, 0, KVH))
        def _():
            val = chip_sum(h, z)
            for k in (1, 2):
                for d in (0, 1):
                    part(h, d, k).wait_recv()
                    val = val + rsr[h, d, k].astype(f32)
            dx, _ = norm_grad(kp[:, cols(h)].astype(f32), kg[...], val[0])
            dkp[:, cols(h)] = dx.astype(bf16)
            dvp[:, cols(h)] = val[1].astype(bf16)

    def reduce(i):
        reduce_end(i - 3)
        reduce_mid(i - 2)
        reduce_start(i - 1)

    base = (0, 2, 10, 14)

    def gain_copy(i, slot_of, src_dev, n):
        return remote(gsend.at[i], grecv.at[slot_of], g_s.at[i, n], g_r.at[slot_of], src_dev)

    def share_gains(i):
        index = stages[i][0][1]
        slot = base[i] + index
        grecv[slot] = gsend[i]
        for n, (_, _, dev) in enumerate(stages[i]):
            gain_copy(i, slot, dev, n).start()

    def sum_gains(i):
        index = stages[i][0][1]
        size = (2, 8, 4, 4)[i]
        for n in range(1, size):
            slot = base[i] + lax.rem(index + n, size)
            gain_copy(i, slot, stages[i][0][2], 0).wait_recv()
        total = grecv[base[i]]
        for n in range(1, size):
            total = total + grecv[base[i] + n]
        return total

    gather_near(0)
    gather_near(1)

    def fill(n, carry):
        part = pl.ds(pl.multiple_of(n * quarter, quarter), quarter)
        pltpu.make_async_copy(q_hbm.at[:, part], qv.at[:, part], q_sem.at[n]).wait()
        prepare(2 * n)
        prepare(2 * n + 1)

        @pl.when(n >= 2)
        def _():
            gather_far(n - 2)

        @pl.when(n == 2)
        def _():
            gather_hop(3, 0)

        return carry

    lax.fori_loop(0, 4, fill, 0)
    gather_near(2)
    pltpu.make_async_copy(do_hbm, dov, do_sem).wait()
    gather_end(0, 0)
    gather_hop(3, 1)
    gather_hop(4, 0)

    def main(i, carry):
        gather_end(i + 1, 2)
        gather_last(i + 1)
        gather_far(i + 2)
        for k in (3, 2, 1, 0):
            gather_hop(i + 5 - k, k)

        def between_halves():
            @pl.when(i == 0)
            def _():
                gather_end(1, 1)

            reduce(i)

        compute(i, between_halves)
        return carry

    lax.fori_loop(0, KVH, main, 0)

    def gain_step(i):
        if i == 0:
            q_sum = jnp.sum(gq[...], axis=0, keepdims=True)
            k_sum = jnp.sum(gk[...], axis=0, keepdims=True)
            row = lax.broadcasted_iota(jnp.int32, (8, HD), 0)
            gsend[0] = jnp.where(row == 0, q_sum, jnp.where(row == 1, k_sum, 0.0))
        else:
            gsend[i] = sum_gains(i - 1)
        share_gains(i)

    def late(n, carry):
        for i in range(4):

            @pl.when(n == i)
            def _(i=i):
                gain_step(i)

        queries(2 * n)
        reduce(KVH + n)
        queries(2 * n + 1)
        return carry

    lax.fori_loop(0, 4, late, 0)
    total = sum_gains(3)
    gq_out[...] = total[0:1]
    gk_out[...] = total[1:2]

    def drain(h, carry):
        for d in (0, 1):
            for k in range(4):
                part(h, d, k).wait_send()
        for k in range(6):
            block(h, mine, ag_s.at[h, k], ag_r.at[h, mine], sibling).wait_send()

        @pl.when(h < EARLY)
        def _():
            for k in (0, 1):
                half_block(h, mine, k, ag_s.at[h, 6 + k], ag_v.at[h], sibling).wait_send()

        @pl.when(h >= EARLY)
        def _():
            block(h, mine, ag_s.at[h, 6], ag_r.at[h, mine], sibling).wait_send()

        for k in range(NZ):
            block(h, mine, ag_b.at[h, k], ag_r.at[h, mine], sibling).wait_send()
        remote(sib.at[h], sib.at[h], sl_s.at[h], sl_r.at[h], sibling).wait_send()
        dq_copy(h).wait()
        return carry

    lax.fori_loop(0, KVH, drain, 0)
    for i in range(4):
        for n, (_, _, dev) in enumerate(stages[i]):
            gain_copy(i, base[i], dev, n).wait_send()


def body(q_raw, d_out, k_prompt, v_prompt, k_comp, v_comp, lengths, q_gain, k_gain):
    vmem = pl.BlockSpec(memory_space=pltpu.VMEM)
    hbm = pl.BlockSpec(memory_space=pl.ANY)
    dma = pltpu.SemaphoreType.DMA
    wide = KVH * HD
    shape = jax.ShapeDtypeStruct
    outs = pl.pallas_call(
        kernel,
        out_shape=(
            shape((SLOTS, GRP * wide), bf16),
            shape((SLOTS, wide), bf16),
            shape((SLOTS, wide), bf16),
            shape((PAGE, wide), bf16),
            shape((PAGE, wide), bf16),
            shape((1, HD), f32),
            shape((1, HD), f32),
        ),
        in_specs=[hbm, hbm] + [vmem] * 7,
        out_specs=[hbm] + [vmem] * 6,
        scratch_shapes=[
            pltpu.VMEM((SLOTS, GRP * wide), bf16),
            pltpu.VMEM((SLOTS, GRP * wide), bf16),
            pltpu.VMEM((KVH, ROWS, 2 * HD), bf16),
            pltpu.VMEM((KVH, SLOTS, HD), bf16),
            pltpu.VMEM((HD, SLOTS), f32),
            pltpu.VMEM((SLOTS, CH), f32),
            pltpu.VMEM((KVH, NB, 2, PAGE, HD), bf16),
            pltpu.VMEM((2, KEYS, CH), f32),
            pltpu.VMEM((2, KEYS, CH), f32),
            pltpu.VMEM((KEYS, HALF), bf16),
            pltpu.VMEM((KVH, KEYS, ROWS), bf16),
            pltpu.VMEM((KEYS, HD), f32),
            pltpu.VMEM((KEYS, 2 * HD), f32),
            pltpu.VMEM((KVH, NB, 2, PAGE, HD), f32),
            pltpu.VMEM((KVH, NZ, 2, PAGE, HD), bf16),
            pltpu.VMEM((KVH, NZ, 2, PAGE, HD), bf16),
            pltpu.VMEM((KVH, 2, 4, 2, PAGE, HD), bf16),
            pltpu.VMEM((KVH, 2, 4, 2, PAGE, HD), bf16),
            pltpu.VMEM((8, HD), f32),
            pltpu.VMEM((8, HD), f32),
            pltpu.VMEM((4, 8, HD), f32),
            pltpu.VMEM((18, 8, HD), f32),
            dma((4,)),
            dma(()),
            dma((KVH,)),
            dma((KVH, 8)),
            dma((KVH, 8)),
            dma((KVH, NB)),
            dma((KVH,)),
            dma((KVH,)),
            dma((KVH,)),
            dma((KVH, 2, 4)),
            dma((KVH, 2, 4)),
            dma((4, 8)),
            dma((18,)),
        ],
        compiler_params=pltpu.CompilerParams(
            collective_id=0, has_side_effects=True, vmem_limit_bytes=60 * 2**20
        ),
        cost_estimate=pl.CostEstimate(flops=13 * 10**9, bytes_accessed=8 * 2**20, transcendentals=10**7),
        name="attention_backward",
    )(
        q_raw[0], d_out[0], k_prompt[0], v_prompt[0], k_comp[0], v_comp[0], lengths[0],
        q_gain.reshape(1, HD), k_gain.reshape(1, HD),
    )
    *large, gq, gk = finish(outs)
    return tuple(x[None] for x in large) + (gq.reshape(HD), gk.reshape(HD))


def finish_kernel(*refs):
    ins, outs, stage, sem_in, sem_out = refs[:7], refs[7:14], refs[14:19], refs[19], refs[20]
    pieces = [(0, pl.ds(i * (SLOTS // 4), SLOTS // 4)) for i in range(4)]
    pieces += [(i, pl.ds(0, ins[i].shape[0])) for i in range(1, 5)]
    loads = [pltpu.make_async_copy(ins[i].at[at], stage[i].at[at], sem_in.at[n]) for n, (i, at) in enumerate(pieces)]
    stores = [pltpu.make_async_copy(stage[i].at[at], outs[i].at[at], sem_out.at[n]) for n, (i, at) in enumerate(pieces)]
    for copy in loads:
        copy.start()
    outs[5][...] = ins[5][...]
    outs[6][...] = ins[6][...]
    for load, store in zip(loads, stores):
        load.wait()
        store.start()
    for copy in stores:
        copy.wait()


def finish(arrays):
    vmem = pl.BlockSpec(memory_space=pltpu.VMEM)
    hbm = pl.BlockSpec(memory_space=pl.ANY)
    return pl.pallas_call(
        finish_kernel,
        out_shape=[jax.ShapeDtypeStruct(x.shape, x.dtype) for x in arrays],
        in_specs=[hbm] * 5 + [vmem] * 2,
        out_specs=[hbm] * 5 + [vmem] * 2,
        scratch_shapes=[pltpu.VMEM(x.shape, x.dtype) for x in arrays[:5]]
        + [pltpu.SemaphoreType.DMA((8,)), pltpu.SemaphoreType.DMA((8,))],
        name="finish",
    )(*arrays)


def solution(mesh):
    split = P("prompt", "comp", None)
    return jax.shard_map(
        body,
        mesh=mesh,
        in_specs=(split,) * 7 + (P(), P()),
        out_specs=(split,) * 5 + (P(), P()),
        check_vma=False,
    )
```
